256 devices in a mesh: sec: 8 (over x, y_lo), ctx: 32 (over z, y_hi, core).
Axes of the slice: x: 4, y: 4 (y_hi: 2, y_lo: 2; y = y_hi * 2 + y_lo), z: 8, core: 2. Of those that a mesh axis runs over, the one named last changes fastest.
Arguments:
- hidden_state: bfloat16 [8, 4096, 4096], P('sec', 'ctx'), may hold values from -8 to 8
- queries: bfloat16 [8, 4096, 4096], P('sec', 'ctx'), may hold values from -6 to 6
- key_vectors: bfloat16 [8, 4096, 4096], P('sec', 'ctx'), may hold values from -4.5 to 4.5
- value_vectors: bfloat16 [8, 4096, 4096], P('sec', 'ctx'), may hold values from -6 to 6
- modulation: float32 [32, 3, 4096], replicated, may hold values from -3 to 3
- down_weight: bfloat16 [4096, 256], replicated, may hold values from -0.09375 to 0.09375
- conv_weight: bfloat16 [3, 3, 3, 256, 256], replicated, may hold values from -0.078125 to 0.078125
- clip_frames: int32 [8], replicated, may hold values from 16 to 64, as said below
- destination: int32 [8], replicated, may hold values from 0 to 7, as said below
- timestep: int32 [8], replicated, may hold values from 0 to 31
Outputs:
- upsampled: bfloat16 [8, 4096, 256], P('sec', 'ctx')
The draws below stay inside these ranges and needn't reach their ends.
Inputs may be any that keep to these rules, and one draw needn't show every extreme that they name: `clip_frames`: one section's clip fills all 64 frames. `destination`: every upsampler group receives exactly one clip; some group d receives the clip of section (d + 4) mod 8.
All inputs are finite; a program needn't handle non-finite values.
Results may differ from the reference program's by a relative error of at most 0.0063.
Values may be sent and summed in bfloat16 or wider, within the bound.
A program may use at most 64 MiB of HBM per device.

```python
import math
import jax
import jax.numpy as jnp
from jax import lax

HEADS = 32
HD = 128
D = 4096
C_UP = 256
HH = 8
WW = 8
STEPS = 32
FRAMES = 64
SEQ = 4096
SECS = 8


def attention_pair(key):
    query_key, other_key = jax.random.split(jax.random.fold_in(key, 7), 2)
    query_rows = jnp.clip(jax.random.normal(query_key, (SECS, SEQ, D), jnp.float32), -4.5, 4.5)
    key_rows = jnp.clip(jax.random.normal(other_key, (SECS, SEQ, D), jnp.float32), -4.5, 4.5)
    return (query_rows, key_rows)


def draw_queries(key, part):
    return attention_pair(key)[0].astype(jnp.bfloat16)


def draw_key_vectors(key, part):
    return attention_pair(key)[1].astype(jnp.bfloat16)


def draw_hidden_state(key, part):
    scale_key, row_key, entry_key = jax.random.split(jax.random.fold_in(key, 11), 3)
    column_scale = jnp.exp(jax.random.uniform(scale_key, (D,), jnp.float32, 0.0, math.log(10.0)))
    row_scale = jnp.exp(jax.random.uniform(row_key, (SECS, SEQ, 1), jnp.float32, 0.0, math.log(10.0)))
    entries = jnp.clip(jax.random.normal(entry_key, (SECS, SEQ, D), jnp.float32), -4.0, 4.0)
    result = 0.02 * row_scale * entries * column_scale
    return jnp.clip(result, -8.0, 8.0).astype(jnp.bfloat16)


def draw_clip_frames(key, part):
    first_key, second_key = jax.random.split(jax.random.fold_in(key, 13))
    lengths = jax.random.randint(first_key, (SECS,), max(1, FRAMES // 4), FRAMES + 1)
    longest = jax.random.randint(second_key, (), 0, SECS)
    return jnp.where(jnp.arange(SECS) == longest, FRAMES, lengths).astype(jnp.int32)


def draw_destination(key, part):
    order_key, pick_key = jax.random.split(jax.random.fold_in(key, 17))
    section_ids = jnp.arange(SECS, dtype=jnp.int32)
    order = jax.random.permutation(order_key, section_ids).astype(jnp.int32)
    target = jax.random.randint(pick_key, (), 0, SECS).astype(jnp.int32)
    sender = ((target + SECS // 2) % SECS).astype(jnp.int32)
    holder = jnp.sum(jnp.where(order == target, section_ids, 0)).astype(jnp.int32)
    displaced = jnp.sum(jnp.where(section_ids == sender, order, 0)).astype(jnp.int32)
    order = jnp.where(section_ids == holder, displaced, order)
    order = jnp.where(section_ids == sender, target, order)
    return order.astype(jnp.int32)


def set_ends(values, stream_key, least, largest):
    extent = values.shape
    place = [jax.random.randint(jax.random.fold_in(stream_key, axis), (), 0, extent[axis]) for axis in range(len(extent))]
    values = values.at[tuple(place)].set(least)
    longest = extent.index(max(extent))
    place[longest] = (place[longest] + 1) % extent[longest]
    return values.at[tuple(place)].set(largest)


def block_levels(own_key, dims, cuts, smallest, top_value):
    def one(axis_at, parts):
        draws = jax.random.uniform(jax.random.fold_in(jax.random.fold_in(own_key, 6), axis_at), (parts,), jnp.float32, smallest / len(cuts), top_value / len(cuts))
        return jnp.repeat(jnp.exp(draws), dims[axis_at] // parts).reshape((-1,) + (1,) * (len(dims) - axis_at - 1))

    gain = one(*cuts[0])
    for cut in cuts[1:]:
        gain = gain * one(*cut)
    return gain


def scatter_about(own_key, dims, width, bound, shards=(), kind=jnp.bfloat16):
    array = jax.random.normal(own_key, dims, jnp.float32) * width
    if len(shards) > 0:
        array = block_levels(own_key, dims, shards, -0.22, 0.18) * array
    return jnp.clip(array, min=-bound, max=bound).astype(kind)


def setup_inputs(seed: int = 0) -> dict:
    splits = jax.random.split(jax.random.key(seed), 11)
    hidden_state = draw_hidden_state(jax.random.fold_in(splits[10], 71), 0)
    queries = draw_queries(jax.random.fold_in(splits[10], 71), 0)
    key_vectors = draw_key_vectors(jax.random.fold_in(splits[10], 71), 0)
    value_vectors = scatter_about(splits[3], (SECS, SEQ, D), 1.0, 6.0, ((0, 8), (1, 32)))
    modulation = scatter_about(splits[4], (STEPS, 3, D), 0.5, 3.0, (), jnp.float32)
    down_weight = scatter_about(splits[5], (D, C_UP), D ** -0.5, 0.09375)
    conv_weight = scatter_about(splits[6], (3, 3, 3, C_UP, C_UP), (27 * C_UP) ** -0.5, 0.078125)
    clip_frames = draw_clip_frames(jax.random.fold_in(splits[10], 71), 0)
    destination = draw_destination(jax.random.fold_in(splits[10], 71), 0)
    timestep = set_ends(jax.random.randint(splits[9], (SECS,), 0, STEPS), jax.random.fold_in(splits[9], 1), 0, STEPS - 1).astype(jnp.int32)
    return {"hidden_state": hidden_state, "queries": queries, "key_vectors": key_vectors, "value_vectors": value_vectors, "modulation": modulation, "down_weight": down_weight, "conv_weight": conv_weight, "clip_frames": clip_frames, "destination": destination, "timestep": timestep}


def head_attention(query_head, key_head, value_head, key_valid):
    block_rows = min(512, SEQ)
    score_scale = 1.0 / math.sqrt(HD)
    query_blocks = query_head.reshape(SEQ // block_rows, block_rows, HD)

    def one_block(query_block):
        scores = jnp.dot(query_block, key_head.T, preferred_element_type=jnp.float32) * score_scale
        scores = jnp.where(key_valid[None, :], scores, -jnp.inf)
        weights = jnp.exp(scores - lax.optimization_barrier(jnp.max(scores, axis=1, keepdims=True)))
        row_total = lax.optimization_barrier(jnp.sum(weights, axis=1, keepdims=True))
        rounded = weights.astype(jnp.bfloat16)
        product = jnp.dot(rounded, value_head, preferred_element_type=jnp.float32)
        return (product / row_total).astype(jnp.bfloat16)
    return lax.map(one_block, query_blocks).reshape(SEQ, HD)

def section_block(hidden_rows, query_rows, key_rows, value_rows, mod_rows, frames, down_weight):
    positions = jnp.arange(SEQ, dtype=jnp.int32) // (HH * WW)
    key_valid = positions < frames

    def by_heads(tensor):
        return tensor.reshape(SEQ, HEADS, HD).transpose(1, 0, 2)

    def one_head(head_inputs):
        return head_attention(head_inputs[0], head_inputs[1], head_inputs[2], key_valid)
    attended = lax.map(one_head, (by_heads(query_rows), by_heads(key_rows), by_heads(value_rows)))
    attended = attended.transpose(1, 0, 2).reshape(SEQ, D)
    block_out = (hidden_rows.astype(jnp.float32) + mod_rows[2] * attended.astype(jnp.float32)).astype(jnp.bfloat16)
    wide_values = block_out.astype(jnp.float32)
    centre = lax.optimization_barrier(jnp.mean(wide_values, axis=-1, keepdims=True))
    spread = lax.optimization_barrier(jnp.mean(jnp.square(wide_values - centre), axis=-1, keepdims=True))
    normed = ((wide_values - centre) * lax.rsqrt(spread + 1e-06) * (1.0 + mod_rows[1]) + mod_rows[0]).astype(jnp.bfloat16)
    return jnp.dot(normed, down_weight, preferred_element_type=jnp.float32).astype(jnp.bfloat16)

def reference(hidden_state, queries, key_vectors, value_vectors, modulation, down_weight, conv_weight, clip_frames, destination, timestep):
    projected_list = []
    for section in range(SECS):
        projected_list.append(section_block(hidden_state[section], queries[section], key_vectors[section], value_vectors[section], modulation[timestep[section]], clip_frames[section], down_weight))
    projected = jnp.stack(projected_list)
    source_of = jnp.argsort(destination)
    positions = jnp.arange(SEQ, dtype=jnp.int32) // (HH * WW)
    outputs = []
    for target in range(SECS):
        source = source_of[target]
        keep_token = (positions < clip_frames[source])[:, None]
        clip_cells = jnp.where(keep_token, projected[source], 0).astype(jnp.bfloat16)
        convolved = lax.conv_general_dilated(clip_cells.reshape(1, FRAMES, HH, WW, C_UP), conv_weight, (1, 1, 1), ((1, 1), (1, 1), (1, 1)), dimension_numbers=('NDHWC', 'DHWIO', 'NDHWC'), preferred_element_type=jnp.float32)
        convolved = convolved.reshape(SEQ, C_UP)
        outputs.append(jnp.where(keep_token, clip_cells.astype(jnp.float32) + convolved, 0.0).astype(jnp.bfloat16))
    return jnp.stack(outputs)
```

```python
import functools
import math

import jax
import jax.numpy as jnp
from jax import lax
from jax.experimental import pallas as pl
from jax.experimental.pallas import tpu as pltpu
from jax.sharding import PartitionSpec as P

HEADS = 32
HD = 128
CELLS = 64
MESH = pl.DeviceIdType.MESH
BF = jnp.bfloat16
F32 = jnp.float32


def kernel(
    frames_ref, dest_ref, step_ref,
    q_hbm, k_hbm, v_hbm, hid_hbm, mod_hbm, down_hbm, conv_hbm,
    out_ref,
    qf, kf, vf, k2, v2, o_send, att, hid, mod, down, conv, proj, xpad, lohalo, hihalo, upbuf, gathered,
    send_k, send_v, send_q, send_o, send_h, send_g,
    recv_k, recv_v, recv_q, recv_o, recv_h, recv_g, w_sem,
):
    rows = q_hbm.shape[0]
    ctx = lax.axis_size("ctx")
    secs = lax.axis_size("sec")
    me = lax.axis_index("ctx")
    sec = lax.axis_index("sec")
    zi, yi, ci = me // 4, (me // 2) % 2, me % 2
    group = 4 * rows
    groups = ctx // 4

    def place(dz, dy, dc):
        return lax.rem(zi + dz, groups) * 4 + lax.rem(yi + dy, 2) * 2 + lax.rem(ci + dc, 2)

    barrier = pltpu.get_barrier_semaphore()

    def greet_ctx(i, carry):
        pl.semaphore_signal(barrier, inc=1, device_id={"ctx": lax.rem(me + i, ctx)}, device_id_type=MESH)
        return carry

    def greet_sec(i, carry):
        pl.semaphore_signal(barrier, inc=1, device_id={"sec": lax.rem(sec + i, secs)}, device_id_type=MESH)
        return carry

    lax.fori_loop(1, ctx, greet_ctx, 0)
    lax.fori_loop(1, secs, greet_sec, 0)
    pl.semaphore_wait(barrier, ctx - 1 + secs - 1)

    my_rows = pl.ds(pl.multiple_of(me * rows, rows), rows)
    my_cols = pl.ds(pl.multiple_of(me * HD, HD), HD)

    def scatter(src, dst, send, recv):
        def one(i, carry):
            k = i // 4
            dz = lax.rem(jnp.where(k % 2 == 0, k // 2 + 1, 7 - k // 2), 8)
            dz = jnp.where(k == 7, 0, dz)
            j = 3 - i % 4
            to = place(dz, j // 2, j % 2)
            cols = pl.ds(pl.multiple_of(to * HD, HD), HD)
            pltpu.make_async_remote_copy(
                src_ref=src.at[:, cols], dst_ref=dst.at[my_rows], send_sem=send, recv_sem=recv,
                device_id={"ctx": to}, device_id_type=MESH,
            ).start()
            return carry

        lax.fori_loop(0, ctx - 1, one, 0)
        pltpu.make_async_copy(src.at[:, my_cols], dst.at[my_rows], recv).start()

    scatter(k_hbm, kf, send_k, recv_k)
    scatter(v_hbm, vf, send_v, recv_v)
    scatter(q_hbm, qf, send_q, recv_q.at[zi])
    loads = [
        pltpu.make_async_copy(a, b, w_sem.at[n])
        for n, (a, b) in enumerate(((hid_hbm, hid), (mod_hbm, mod), (down_hbm, down), (conv_hbm, conv)))
    ]
    for load in loads:
        load.start()

    frames = frames_ref[sec]
    pltpu.make_async_copy(kf, kf, recv_k).wait()
    first = kf[0:1, :]
    key_at = lax.broadcasted_iota(jnp.int32, kf.shape, 0)
    valid = key_at < frames * CELLS
    kk = jnp.where(valid, kf[...].astype(F32), first.astype(F32)).astype(BF)
    k2[:, 0:HD] = kk
    k2[:, HD:] = kk
    pltpu.make_async_copy(vf, vf, recv_v).wait()
    v2[:, 0:HD] = jnp.where(valid, vf[...].astype(F32), 0.0).astype(BF)
    v2[:, HD:] = jnp.where(valid, 1.0, 0.0).astype(BF)

    scale = math.log2(math.e) / math.sqrt(HD)

    def attend(k, carry):
        dz = lax.rem(jnp.where(k % 2 == 0, 4 - k // 2, 5 + k // 2), groups)
        g = lax.rem(zi + dz, groups)
        at = pl.ds(pl.multiple_of(g * group, group), group)
        pltpu.make_async_copy(qf.at[at], qf.at[at], recv_q.at[g]).wait()
        wide = qf[at, :].astype(F32) * scale
        high = wide.astype(BF)
        low = (wide - high.astype(F32)).astype(BF)
        q2 = jnp.concatenate([high, low], axis=1)
        scores = lax.dot_general(q2, k2[...], (((1,), (1,)), ((), ())), preferred_element_type=F32)
        top = jnp.max(scores, axis=1, keepdims=True)
        weights = jnp.exp2(scores - top).astype(BF)
        both = jnp.dot(weights, v2[...], preferred_element_type=F32)
        o_send[at, :] = (both[:, 0:HD] / both[:, HD:]).astype(BF)
        for j in (3, 2, 1, 0):
            to = place(dz, j // 2, j % 2)
            block = o_send.at[pl.ds(pl.multiple_of(to * rows, rows), rows)]

            def remote(to=to, block=block):
                pltpu.make_async_remote_copy(
                    src_ref=block, dst_ref=att.at[:, my_cols], send_sem=send_o, recv_sem=recv_o,
                    device_id={"ctx": to}, device_id_type=MESH,
                ).start()

            if j:
                remote()
            else:
                pl.when(k < groups - 1)(remote)
        return carry

    lax.fori_loop(0, groups, attend, 0)
    pltpu.make_async_copy(o_send.at[my_rows], att.at[:, my_cols], recv_o).start()

    for load in loads:
        load.wait()
    now = step_ref[sec]
    shift, scale_up, gate = (mod[n, pl.ds(now, 1), :] for n in range(3))
    pltpu.make_async_copy(att, att, recv_o).wait()
    block = (hid[...].astype(F32) + gate * att[...].astype(F32)).astype(BF)
    wide = block.astype(F32)
    centre = jnp.mean(wide, axis=1, keepdims=True)
    away = wide - centre
    spread = jnp.mean(away * away, axis=1, keepdims=True)
    normed = (away * lax.rsqrt(spread + 1e-06) * (1.0 + scale_up) + shift).astype(BF)
    projected = jnp.dot(normed, down[...], preferred_element_type=F32).astype(BF)
    cell = me * rows + lax.broadcasted_iota(jnp.int32, projected.shape, 0)
    keep = cell < frames * CELLS
    clip = jnp.where(keep, projected.astype(F32), 0.0)
    proj[...] = clip.astype(BF)

    below = lax.rem(me + ctx - 1, ctx)
    above = lax.rem(me + 1, ctx)
    up = pltpu.make_async_remote_copy(
        src_ref=proj.at[pl.ds(rows - CELLS, CELLS)], dst_ref=lohalo, send_sem=send_h.at[0], recv_sem=recv_h.at[0],
        device_id={"ctx": above}, device_id_type=MESH)
    dn = pltpu.make_async_remote_copy(
        src_ref=proj.at[pl.ds(0, CELLS)], dst_ref=hihalo, send_sem=send_h.at[1], recv_sem=recv_h.at[1],
        device_id={"ctx": below}, device_id_type=MESH)
    up.start()
    dn.start()
    up.wait_recv()
    dn.wait_recv()

    total_rows = rows + 2 * CELLS
    xpad[0:CELLS, :] = jnp.where(me > 0, lohalo[...].astype(F32), 0.0)
    xpad[CELLS:CELLS + rows, :] = clip
    xpad[CELLS + rows:, :] = jnp.where(me < ctx - 1, hihalo[...].astype(F32), 0.0)
    padded = xpad[...]
    at = lax.broadcasted_iota(jnp.int32, padded.shape, 0) % CELLS
    row, col = at // 8, at % 8
    total = clip
    for b in range(3):
        for e in range(3):
            step = (b - 1) * 8 + (e - 1)
            moved = padded if step == 0 else pltpu.roll(padded, (-step) % total_rows, 0)
            inside = (row + b - 1 >= 0) & (row + b - 1 < 8) & (col + e - 1 >= 0) & (col + e - 1 < 8)
            moved = jnp.where(inside, moved, 0.0).astype(BF)
            for a in range(3):
                total += jnp.dot(moved[a * CELLS:a * CELLS + rows], conv[a * 9 + b * 3 + e], preferred_element_type=F32)
    upbuf[...] = jnp.where(keep, total, 0.0).astype(BF)

    def spread_out(i, carry):
        pltpu.make_async_remote_copy(
            src_ref=upbuf, dst_ref=gathered.at[sec], send_sem=send_g, recv_sem=recv_g,
            device_id={"sec": lax.rem(sec + i, secs)}, device_id_type=MESH,
        ).start()
        return carry

    lax.fori_loop(1, secs, spread_out, 0)
    pltpu.make_async_copy(upbuf, gathered.at[sec], recv_g).start()

    source = jnp.int32(0)
    for s in range(dest_ref.shape[0]):
        source = jnp.where(dest_ref[s] == sec, s, source)
    others = pl.ds(0, (ctx - 1) * rows)
    pltpu.make_async_copy(kf.at[others], kf.at[others], send_k).wait()
    pltpu.make_async_copy(vf.at[others], vf.at[others], send_v).wait()
    pltpu.make_async_copy(qf.at[others], qf.at[others], send_q).wait()
    pltpu.make_async_copy(o_send.at[others], o_send.at[others], send_o).wait()
    up.wait_send()
    dn.wait_send()
    sent = pl.ds(0, secs - 1)
    pltpu.make_async_copy(gathered.at[sent], gathered.at[sent], send_g).wait()
    pltpu.make_async_copy(gathered, gathered, recv_g).wait()
    out_ref[...] = gathered[source]


def body(hidden, queries, keys, values, modulation, down_weight, conv_weight, clip_frames, destination, timestep):
    _, rows, width = queries.shape
    seq = rows * lax.axis_size("ctx")
    secs = lax.axis_size("sec")
    groups = lax.axis_size("ctx") // 4
    up = down_weight.shape[1]
    flat = lambda t: t.reshape(rows, width)
    smem = pl.BlockSpec(memory_space=pltpu.SMEM)
    anywhere = pl.BlockSpec(memory_space=pl.ANY)
    dma = pltpu.SemaphoreType.DMA
    taps = conv_weight.reshape(27, up, up)
    modulation = jnp.swapaxes(modulation, 0, 1)
    out = pl.pallas_call(
        kernel,
        out_shape=jax.ShapeDtypeStruct((rows, up), BF),
        in_specs=[smem] * 3 + [anywhere] * 7,
        out_specs=pl.BlockSpec(memory_space=pltpu.VMEM),
        scratch_shapes=[
            pltpu.VMEM((seq, HD), BF), pltpu.VMEM((seq, HD), BF), pltpu.VMEM((seq, HD), BF),
            pltpu.VMEM((seq, 2 * HD), BF), pltpu.VMEM((seq, 2 * HD), BF),
            pltpu.VMEM((seq, HD), BF), pltpu.VMEM((rows, width), BF), pltpu.VMEM((rows, width), BF),
            pltpu.VMEM(modulation.shape, F32), pltpu.VMEM(down_weight.shape, BF), pltpu.VMEM(taps.shape, BF),
            pltpu.VMEM((rows, up), BF), pltpu.VMEM((rows + 2 * CELLS, up), F32),
            pltpu.VMEM((CELLS, up), BF), pltpu.VMEM((CELLS, up), BF),
            pltpu.VMEM((rows, up), BF), pltpu.VMEM((secs, rows, up), BF),
            dma, dma, dma, dma, dma((2,)), dma,
            dma, dma, dma((groups,)), dma, dma((2,)), dma, dma((4,)),
        ],
        compiler_params=pltpu.CompilerParams(
            collective_id=0, has_side_effects=True, vmem_limit_bytes=60 << 20
        ),
        name="section_kernel",
    )(clip_frames, destination, timestep, flat(queries), flat(keys), flat(values), flat(hidden), modulation, down_weight, taps)
    return out.reshape(1, rows, up)


def solution(mesh):
    tokens = P("sec", "ctx", None)
    return jax.shard_map(
        body, mesh=mesh, in_specs=(tokens,) * 4 + (P(),) * 6, out_specs=tokens, check_vma=False
    )
```

```python
import functools
import math

import jax
import jax.numpy as jnp
from jax import lax
from jax.experimental import pallas as pl
from jax.experimental.pallas import tpu as pltpu
from jax.sharding import PartitionSpec as P

HEADS = 32
HD = 128
CELLS = 64
SUB = 256
MESH = pl.DeviceIdType.MESH
BF = jnp.bfloat16
F32 = jnp.float32


def kernel(
    frames_ref, dest_ref, step_ref,
    q_hbm, k_hbm, v_hbm, hid_hbm, mod_hbm, down_hbm, conv_hbm,
    out_ref,
    qf, kf, vf, k2, v2, o_send, att, hid, mod, down, conv, proj, xpad, lohalo, hihalo, upbuf, gathered, scores,
    send_k, send_v, send_q, send_o, send_h, send_g,
    recv_k, recv_v, recv_q, recv_o, recv_h, recv_g, w_sem,
):
    rows = q_hbm.shape[0]
    ctx = lax.axis_size("ctx")
    secs = lax.axis_size("sec")
    me = lax.axis_index("ctx")
    sec = lax.axis_index("sec")
    zi, yi, ci = me // 4, (me // 2) % 2, me % 2
    group = 4 * rows
    groups = ctx // 4

    def place(dz, dy, dc):
        return lax.rem(zi + dz, groups) * 4 + lax.rem(yi + dy, 2) * 2 + lax.rem(ci + dc, 2)

    barrier = pltpu.get_barrier_semaphore()

    def greet_ctx(i, carry):
        pl.semaphore_signal(barrier, inc=1, device_id={"ctx": lax.rem(me + i, ctx)}, device_id_type=MESH)
        return carry

    def greet_sec(i, carry):
        pl.semaphore_signal(barrier, inc=1, device_id={"sec": lax.rem(sec + i, secs)}, device_id_type=MESH)
        return carry

    lax.fori_loop(1, ctx, greet_ctx, 0)
    lax.fori_loop(1, secs, greet_sec, 0)
    pl.semaphore_wait(barrier, ctx - 1 + secs - 1)

    def offset(k):
        half = groups // 2
        return lax.rem(jnp.where(k % 2 == 0, half - k // 2, half + 1 + k // 2), groups)

    my_rows = pl.ds(pl.multiple_of(me * rows, rows), rows)
    my_cols = pl.ds(pl.multiple_of(me * HD, HD), HD)

    def scatter(src, dst, send, recv):
        def one(i, carry):
            dz, j = lax.rem(groups - offset(i // 4), groups), 3 - i % 4
            to = place(dz, j // 2, j % 2)
            cols = pl.ds(pl.multiple_of(to * HD, HD), HD)
            pltpu.make_async_remote_copy(
                src_ref=src.at[:, cols], dst_ref=dst.at[my_rows], send_sem=send, recv_sem=recv,
                device_id={"ctx": to}, device_id_type=MESH,
            ).start()
            return carry

        lax.fori_loop(0, ctx - 1, one, 0)
        pltpu.make_async_copy(src.at[:, my_cols], dst.at[my_rows], recv).start()

    scatter(k_hbm, kf, send_k, recv_k)
    scatter(v_hbm, vf, send_v, recv_v)
    scatter(q_hbm, qf, send_q, recv_q.at[zi])
    loads = [
        pltpu.make_async_copy(a, b, w_sem.at[n])
        for n, (a, b) in enumerate(((hid_hbm, hid), (mod_hbm, mod), (down_hbm, down), (conv_hbm, conv)))
    ]
    for load in loads:
        load.start()

    frames = frames_ref[sec]
    pltpu.make_async_copy(kf, kf, recv_k).wait()
    first = kf[0:1, :]
    key_at = lax.broadcasted_iota(jnp.int32, kf.shape, 0)
    valid = key_at < frames * CELLS
    kk = jnp.where(valid, kf[...].astype(F32), first.astype(F32)).astype(BF)
    k2[:, 0:HD] = kk
    k2[:, HD:] = kk
    pltpu.make_async_copy(vf, vf, recv_v).wait()
    v2[:, 0:HD] = jnp.where(valid, vf[...].astype(F32), 0.0).astype(BF)
    v2[:, HD:] = jnp.where(valid, 1.0, 0.0).astype(BF)

    scale = math.log2(math.e) / math.sqrt(HD)

    def attend(k, carry):
        dz = offset(k)
        g = lax.rem(zi + dz, groups)
        at = pl.ds(pl.multiple_of(g * group, group), group)
        pltpu.make_async_copy(qf.at[at], qf.at[at], recv_q.at[g]).wait()
        start = g * group

        def part(i):
            return pl.ds(pl.multiple_of(start + i * SUB, SUB), SUB)

        def score(i):
            wide = qf[part(i), :].astype(F32) * scale
            high = wide.astype(BF)
            low = (wide - high.astype(F32)).astype(BF)
            q2 = jnp.concatenate([high, low], axis=1)
            return lax.dot_general(q2, k2[...], (((1,), (1,)), ((), ())), preferred_element_type=F32)

        parts = group // SUB
        scores[0] = score(0)
        for i in range(parts):
            if i + 1 < parts:
                scores[(i + 1) % 2] = score(i + 1)
            here = scores[i % 2]
            top = jnp.max(here, axis=1, keepdims=True)
            weights = jnp.exp2(here - top).astype(BF)
            both = jnp.dot(weights, v2[...], preferred_element_type=F32)
            o_send[part(i), :] = (both[:, 0:HD] / both[:, HD:]).astype(BF)
        for j in (3, 2, 1, 0):
            to = place(dz, j // 2, j % 2)
            block = o_send.at[pl.ds(pl.multiple_of(to * rows, rows), rows)]

            def remote(to=to, block=block):
                pltpu.make_async_remote_copy(
                    src_ref=block, dst_ref=att.at[:, my_cols], send_sem=send_o, recv_sem=recv_o,
                    device_id={"ctx": to}, device_id_type=MESH,
                ).start()

            if j:
                remote()
            else:
                pl.when(k < groups - 1)(remote)
        return carry

    lax.fori_loop(0, groups, attend, 0)
    pltpu.make_async_copy(o_send.at[my_rows], att.at[:, my_cols], recv_o).start()

    for load in loads:
        load.wait()
    now = step_ref[sec]
    shift, scale_up, gate = (mod[n, pl.ds(now, 1), :] for n in range(3))
    pltpu.make_async_copy(att, att, recv_o).wait()
    block = (hid[...].astype(F32) + gate * att[...].astype(F32)).astype(BF)
    wide = block.astype(F32)
    centre = jnp.mean(wide, axis=1, keepdims=True)
    away = wide - centre
    spread = jnp.mean(away * away, axis=1, keepdims=True)
    normed = (away * lax.rsqrt(spread + 1e-06) * (1.0 + scale_up) + shift).astype(BF)
    projected = jnp.dot(normed, down[...], preferred_element_type=F32).astype(BF)
    cell = me * rows + lax.broadcasted_iota(jnp.int32, projected.shape, 0)
    keep = cell < frames * CELLS
    clip = jnp.where(keep, projected.astype(F32), 0.0)
    proj[...] = clip.astype(BF)

    below = lax.rem(me + ctx - 1, ctx)
    above = lax.rem(me + 1, ctx)
    up = pltpu.make_async_remote_copy(
        src_ref=proj.at[pl.ds(rows - CELLS, CELLS)], dst_ref=lohalo, send_sem=send_h.at[0], recv_sem=recv_h.at[0],
        device_id={"ctx": above}, device_id_type=MESH)
    dn = pltpu.make_async_remote_copy(
        src_ref=proj.at[pl.ds(0, CELLS)], dst_ref=hihalo, send_sem=send_h.at[1], recv_sem=recv_h.at[1],
        device_id={"ctx": below}, device_id_type=MESH)
    up.start()
    dn.start()
    up.wait_recv()
    dn.wait_recv()

    total_rows = rows + 2 * CELLS
    xpad[0:CELLS, :] = jnp.where(me > 0, lohalo[...].astype(F32), 0.0)
    xpad[CELLS:CELLS + rows, :] = clip
    xpad[CELLS + rows:, :] = jnp.where(me < ctx - 1, hihalo[...].astype(F32), 0.0)
    padded = xpad[...]
    at = lax.broadcasted_iota(jnp.int32, padded.shape, 0) % CELLS
    row, col = at // 8, at % 8
    total = clip
    for b in range(3):
        for e in range(3):
            step = (b - 1) * 8 + (e - 1)
            moved = padded if step == 0 else pltpu.roll(padded, (-step) % total_rows, 0)
            inside = (row + b - 1 >= 0) & (row + b - 1 < 8) & (col + e - 1 >= 0) & (col + e - 1 < 8)
            moved = jnp.where(inside, moved, 0.0).astype(BF)
            for a in range(3):
                total += jnp.dot(moved[a * CELLS:a * CELLS + rows], conv[a * 9 + b * 3 + e], preferred_element_type=F32)
    upbuf[...] = jnp.where(keep, total, 0.0).astype(BF)

    def spread_out(i, carry):
        pltpu.make_async_remote_copy(
            src_ref=upbuf, dst_ref=gathered.at[sec], send_sem=send_g, recv_sem=recv_g,
            device_id={"sec": lax.rem(sec + i, secs)}, device_id_type=MESH,
        ).start()
        return carry

    lax.fori_loop(1, secs, spread_out, 0)
    pltpu.make_async_copy(upbuf, gathered.at[sec], recv_g).start()

    source = jnp.int32(0)
    for s in range(dest_ref.shape[0]):
        source = jnp.where(dest_ref[s] == sec, s, source)
    others = pl.ds(0, (ctx - 1) * rows)
    pltpu.make_async_copy(kf.at[others], kf.at[others], send_k).wait()
    pltpu.make_async_copy(vf.at[others], vf.at[others], send_v).wait()
    pltpu.make_async_copy(qf.at[others], qf.at[others], send_q).wait()
    pltpu.make_async_copy(o_send.at[others], o_send.at[others], send_o).wait()
    up.wait_send()
    dn.wait_send()
    sent = pl.ds(0, secs - 1)
    pltpu.make_async_copy(gathered.at[sent], gathered.at[sent], send_g).wait()
    pltpu.make_async_copy(gathered, gathered, recv_g).wait()
    out_ref[...] = gathered[source]


def body(hidden, queries, keys, values, modulation, down_weight, conv_weight, clip_frames, destination, timestep):
    _, rows, width = queries.shape
    seq = rows * lax.axis_size("ctx")
    secs = lax.axis_size("sec")
    groups = lax.axis_size("ctx") // 4
    up = down_weight.shape[1]
    flat = lambda t: t.reshape(rows, width)
    smem = pl.BlockSpec(memory_space=pltpu.SMEM)
    anywhere = pl.BlockSpec(memory_space=pl.ANY)
    dma = pltpu.SemaphoreType.DMA
    taps = conv_weight.reshape(27, up, up)
    modulation = jnp.swapaxes(modulation, 0, 1)
    out = pl.pallas_call(
        kernel,
        out_shape=jax.ShapeDtypeStruct((rows, up), BF),
        in_specs=[smem] * 3 + [anywhere] * 7,
        out_specs=pl.BlockSpec(memory_space=pltpu.VMEM),
        scratch_shapes=[
            pltpu.VMEM((seq, HD), BF), pltpu.VMEM((seq, HD), BF), pltpu.VMEM((seq, HD), BF),
            pltpu.VMEM((seq, 2 * HD), BF), pltpu.VMEM((seq, 2 * HD), BF),
            pltpu.VMEM((seq, HD), BF), pltpu.VMEM((rows, width), BF), pltpu.VMEM((rows, width), BF),
            pltpu.VMEM(modulation.shape, F32), pltpu.VMEM(down_weight.shape, BF), pltpu.VMEM(taps.shape, BF),
            pltpu.VMEM((rows, up), BF), pltpu.VMEM((rows + 2 * CELLS, up), F32),
            pltpu.VMEM((CELLS, up), BF), pltpu.VMEM((CELLS, up), BF),
            pltpu.VMEM((rows, up), BF), pltpu.VMEM((secs, rows, up), BF),
            pltpu.VMEM((2, SUB, seq), F32),
            dma, dma, dma, dma, dma((2,)), dma,
            dma, dma, dma((groups,)), dma, dma((2,)), dma, dma((4,)),
        ],
        compiler_params=pltpu.CompilerParams(
            collective_id=0, has_side_effects=True, vmem_limit_bytes=60 << 20
        ),
        name="section_kernel",
    )(clip_frames, destination, timestep, flat(queries), flat(keys), flat(values), flat(hidden), modulation, down_weight, taps)
    return out.reshape(1, rows, up)


def solution(mesh):
    tokens = P("sec", "ctx", None)
    return jax.shard_map(
        body, mesh=mesh, in_specs=(tokens,) * 4 + (P(),) * 6, out_specs=tokens, check_vma=False
    )
```

```python
import functools
import math

import jax
import jax.numpy as jnp
from jax import lax
from jax.experimental import pallas as pl
from jax.experimental.pallas import tpu as pltpu
from jax.sharding import PartitionSpec as P

HEADS = 32
HD = 128
CELLS = 64
SUB = 256
LATE = 32
MESH = pl.DeviceIdType.MESH
BF = jnp.bfloat16
F32 = jnp.float32


def kernel(
    frames_ref, dest_ref, step_ref,
    q_hbm, k_hbm, v_hbm, hid_hbm, mod_hbm, down_hbm, conv_hbm,
    out_ref,
    qf, kf, vf, k2, v2, o_send, att, hid, mod, down, conv, proj, xpad, lohalo, hihalo, last_halo, clip_own, gathered_0, gathered_1, scores,
    send_k, send_v, send_q, send_o, send_h, send_g,
    recv_k, recv_v, recv_q, recv_o, recv_h, recv_g, w_sem,
):
    rows = q_hbm.shape[0]
    ctx = lax.axis_size("ctx")
    secs = lax.axis_size("sec")
    me = lax.axis_index("ctx")
    sec = lax.axis_index("sec")
    below = lax.rem(me + ctx - 1, ctx)
    above = lax.rem(me + 1, ctx)
    zi, yi, ci = me // 4, (me // 2) % 2, me % 2
    parts = ((0, rows - LATE), (rows - LATE, LATE))
    last = len(parts) - 1
    group = 4 * rows
    groups = ctx // 4

    def place(dz, dy, dc):
        return lax.rem(zi + dz, groups) * 4 + lax.rem(yi + dy, 2) * 2 + lax.rem(ci + dc, 2)

    barrier = pltpu.get_barrier_semaphore()

    def greet_ctx(i, carry):
        pl.semaphore_signal(barrier, inc=1, device_id={"ctx": lax.rem(me + i, ctx)}, device_id_type=MESH)
        return carry

    def greet_sec(i, carry):
        for place_at in (me, above, below):
            pl.semaphore_signal(
                barrier, inc=1, device_id={"sec": lax.rem(sec + i, secs), "ctx": place_at}, device_id_type=MESH)
        return carry

    lax.fori_loop(1, ctx, greet_ctx, 0)
    lax.fori_loop(1, secs, greet_sec, 0)
    pl.semaphore_wait(barrier, ctx - 1 + 3 * (secs - 1))

    def offset(k):
        half = groups // 2
        return lax.rem(jnp.where(k % 2 == 0, half - k // 2, half + 1 + k // 2), groups)

    my_rows = pl.ds(pl.multiple_of(me * rows, rows), rows)
    my_cols = pl.ds(pl.multiple_of(me * HD, HD), HD)

    def scatter(src, dst, send, recv):
        def one(i, carry):
            dz, j = lax.rem(groups - offset(i // 4), groups), 3 - i % 4
            to = place(dz, j // 2, j % 2)
            cols = pl.ds(pl.multiple_of(to * HD, HD), HD)
            pltpu.make_async_remote_copy(
                src_ref=src.at[:, cols], dst_ref=dst.at[my_rows], send_sem=send, recv_sem=recv,
                device_id={"ctx": to}, device_id_type=MESH,
            ).start()
            return carry

        lax.fori_loop(0, ctx - 1, one, 0)
        pltpu.make_async_copy(src.at[:, my_cols], dst.at[my_rows], recv).start()

    scatter(k_hbm, kf, send_k, recv_k)
    scatter(v_hbm, vf, send_v, recv_v)
    scatter(q_hbm, qf, send_q, recv_q.at[zi])
    loads = [
        pltpu.make_async_copy(a, b, w_sem.at[n])
        for n, (a, b) in enumerate(((hid_hbm, hid), (mod_hbm, mod), (down_hbm, down), (conv_hbm, conv)))
    ]
    for load in loads:
        load.start()

    frames = frames_ref[sec]
    pltpu.make_async_copy(kf, kf, recv_k).wait()
    first = kf[0:1, :]
    key_at = lax.broadcasted_iota(jnp.int32, kf.shape, 0)
    valid = key_at < frames * CELLS
    kk = jnp.where(valid, kf[...].astype(F32), first.astype(F32)).astype(BF)
    k2[:, 0:HD] = kk
    k2[:, HD:] = kk
    pltpu.make_async_copy(vf, vf, recv_v).wait()
    v2[:, 0:HD] = jnp.where(valid, vf[...].astype(F32), 0.0).astype(BF)
    v2[:, HD:] = jnp.where(valid, 1.0, 0.0).astype(BF)

    scale = math.log2(math.e) / math.sqrt(HD)

    def attend(k, carry):
        dz = offset(k)
        g = lax.rem(zi + dz, groups)
        at = pl.ds(pl.multiple_of(g * group, group), group)
        pltpu.make_async_copy(qf.at[at], qf.at[at], recv_q.at[g]).wait()
        start = g * group

        def part(i):
            return pl.ds(pl.multiple_of(start + i * SUB, SUB), SUB)

        def score(i):
            wide = qf[part(i), :].astype(F32) * scale
            high = wide.astype(BF)
            low = (wide - high.astype(F32)).astype(BF)
            q2 = jnp.concatenate([high, low], axis=1)
            return lax.dot_general(q2, k2[...], (((1,), (1,)), ((), ())), preferred_element_type=F32)

        parts = group // SUB
        scores[0] = score(0)
        for i in range(parts):
            if i + 1 < parts:
                scores[(i + 1) % 2] = score(i + 1)
            here = scores[i % 2]
            top = jnp.max(here, axis=1, keepdims=True)
            weights = jnp.exp2(here - top).astype(BF)
            both = jnp.dot(weights, v2[...], preferred_element_type=F32)
            o_send[part(i), :] = (both[:, 0:HD] / both[:, HD:]).astype(BF)
        for j in (3, 2, 1, 0):
            if j:
                give(0, dz, j)
            else:
                pl.when(k < groups - 1)(functools.partial(give, 0, dz, j))
        return carry

    def give(h, dz, j):
        to = place(dz, j // 2, j % 2)
        start, size = parts[h]
        pltpu.make_async_remote_copy(
            src_ref=o_send.at[pl.ds(pl.multiple_of(to * rows + start, 16), size)],
            dst_ref=att.at[pl.ds(start, size), my_cols],
            send_sem=send_o, recv_sem=recv_o.at[h],
            device_id={"ctx": to}, device_id_type=MESH,
        ).start()

    def keep_own(h):
        start, size = parts[h]
        pltpu.make_async_copy(
            o_send.at[pl.ds(pl.multiple_of(me * rows + start, 16), size)],
            att.at[pl.ds(start, size), my_cols], recv_o.at[h]).start()

    lax.fori_loop(0, groups, attend, 0)
    keep_own(0)
    for h in range(1, len(parts)):
        def rest(i, carry, h=h):
            give(h, offset(i // 4), 3 - i % 4)
            return carry

        lax.fori_loop(0, ctx - 1, rest, 0)
        keep_own(h)

    for load in loads:
        load.wait()
    now = step_ref[sec]
    shift, scale_up, gate = (mod[n, pl.ds(now, 1), :] for n in range(3))
    source = jnp.int32(0)
    for s in range(dest_ref.shape[0]):
        source = jnp.where(dest_ref[s] == sec, s, source)

    def adapt(h):
        start, size = parts[h]
        at = pl.ds(start, size)
        pltpu.make_async_copy(att.at[at], att.at[at], recv_o.at[h]).wait()
        block = (hid[at, :].astype(F32) + gate * att[at, :].astype(F32)).astype(BF)
        wide = block.astype(F32)
        centre = jnp.mean(wide, axis=1, keepdims=True)
        away = wide - centre
        spread = jnp.mean(away * away, axis=1, keepdims=True)
        normed = (away * lax.rsqrt(spread + 1e-06) * (1.0 + scale_up) + shift).astype(BF)
        projected = jnp.dot(normed, down[...], preferred_element_type=F32)
        cell = me * rows + start + lax.broadcasted_iota(jnp.int32, projected.shape, 0)
        proj[at, :] = jnp.where(cell < frames * CELLS, projected, 0.0).astype(BF)

    boxes = (gathered_0, gathered_1)

    def hand_off(h):
        at = pl.ds(*parts[h])

        def one(i, carry):
            pltpu.make_async_remote_copy(
                src_ref=proj.at[at], dst_ref=boxes[h].at[sec], send_sem=send_g.at[h], recv_sem=recv_g.at[h],
                device_id={"sec": lax.rem(sec + i, secs)}, device_id_type=MESH,
            ).start()
            return carry

        def beside(i, carry):
            pltpu.make_async_remote_copy(
                src_ref=proj.at[at], dst_ref=last_halo.at[sec], send_sem=send_h.at[2], recv_sem=recv_h.at[2],
                device_id={"sec": lax.rem(sec + i, secs), "ctx": above}, device_id_type=MESH,
            ).start()
            return carry

        if h == last:
            lax.fori_loop(0, secs, beside, 0)
        lax.fori_loop(1, secs, one, 0)
        pltpu.make_async_copy(proj.at[at], boxes[h].at[sec], recv_g.at[h]).start()

    def take(h):
        pltpu.make_async_copy(boxes[h], boxes[h], recv_g.at[h]).wait()
        clip_own[pl.ds(*parts[h]), :] = boxes[h][source]

    before = CELLS - LATE
    dn = pltpu.make_async_remote_copy(
        src_ref=clip_own.at[pl.ds(0, CELLS)], dst_ref=hihalo, send_sem=send_h.at[0], recv_sem=recv_h.at[0],
        device_id={"ctx": below}, device_id_type=MESH)
    up = before and pltpu.make_async_remote_copy(
        src_ref=clip_own.at[pl.ds(rows - CELLS, before)], dst_ref=lohalo, send_sem=send_h.at[1], recv_sem=recv_h.at[1],
        device_id={"ctx": above}, device_id_type=MESH)

    adapt(0)
    hand_off(0)
    adapt(1)
    hand_off(1)
    take(0)
    dn.start()
    if before:
        up.start()
    take(1)
    dn.wait_recv()
    if before:
        up.wait_recv()
    pltpu.make_async_copy(last_halo, last_halo, recv_h.at[2]).wait()

    total_rows = rows + 2 * CELLS
    clip = clip_own[...].astype(F32)
    if before:
        xpad[0:before, :] = jnp.where(me > 0, lohalo[...].astype(F32), 0.0)
    xpad[before:CELLS, :] = jnp.where(me > 0, last_halo[source].astype(F32), 0.0)
    xpad[CELLS:CELLS + rows, :] = clip
    xpad[CELLS + rows:, :] = jnp.where(me < ctx - 1, hihalo[...].astype(F32), 0.0)
    padded = xpad[...]
    at = lax.broadcasted_iota(jnp.int32, padded.shape, 0) % CELLS
    row, col = at // 8, at % 8
    total = clip
    for b in range(3):
        for e in range(3):
            step = (b - 1) * 8 + (e - 1)
            moved = padded if step == 0 else pltpu.roll(padded, (-step) % total_rows, 0)
            inside = (row + b - 1 >= 0) & (row + b - 1 < 8) & (col + e - 1 >= 0) & (col + e - 1 < 8)
            moved = jnp.where(inside, moved, 0.0).astype(BF)
            for a in range(3):
                total += jnp.dot(moved[a * CELLS:a * CELLS + rows], conv[a * 9 + b * 3 + e], preferred_element_type=F32)
    cell = me * rows + lax.broadcasted_iota(jnp.int32, total.shape, 0)
    out_ref[...] = jnp.where(cell < frames_ref[source] * CELLS, total, 0.0).astype(BF)

    others = pl.ds(0, (ctx - 1) * rows)
    pltpu.make_async_copy(kf.at[others], kf.at[others], send_k).wait()
    pltpu.make_async_copy(vf.at[others], vf.at[others], send_v).wait()
    pltpu.make_async_copy(qf.at[others], qf.at[others], send_q).wait()
    pltpu.make_async_copy(o_send.at[others], o_send.at[others], send_o).wait()
    dn.wait_send()
    if before:
        up.wait_send()
    pltpu.make_async_copy(last_halo, last_halo, send_h.at[2]).wait()
    sent = pl.ds(0, secs - 1)
    for h, box in enumerate(boxes):
        pltpu.make_async_copy(box.at[sent], box.at[sent], send_g.at[h]).wait()


def body(hidden, queries, keys, values, modulation, down_weight, conv_weight, clip_frames, destination, timestep):
    _, rows, width = queries.shape
    seq = rows * lax.axis_size("ctx")
    secs = lax.axis_size("sec")
    groups = lax.axis_size("ctx") // 4
    up = down_weight.shape[1]
    late = min(LATE, CELLS)
    flat = lambda t: t.reshape(rows, width)
    smem = pl.BlockSpec(memory_space=pltpu.SMEM)
    anywhere = pl.BlockSpec(memory_space=pl.ANY)
    dma = pltpu.SemaphoreType.DMA
    taps = conv_weight.reshape(27, up, up)
    modulation = jnp.swapaxes(modulation, 0, 1)
    out = pl.pallas_call(
        kernel,
        out_shape=jax.ShapeDtypeStruct((rows, up), BF),
        in_specs=[smem] * 3 + [anywhere] * 7,
        out_specs=pl.BlockSpec(memory_space=pltpu.VMEM),
        scratch_shapes=[
            pltpu.VMEM((seq, HD), BF), pltpu.VMEM((seq, HD), BF), pltpu.VMEM((seq, HD), BF),
            pltpu.VMEM((seq, 2 * HD), BF), pltpu.VMEM((seq, 2 * HD), BF),
            pltpu.VMEM((seq, HD), BF), pltpu.VMEM((rows, width), BF), pltpu.VMEM((rows, width), BF),
            pltpu.VMEM(modulation.shape, F32), pltpu.VMEM(down_weight.shape, BF), pltpu.VMEM(taps.shape, BF),
            pltpu.VMEM((rows, up), BF), pltpu.VMEM((rows + 2 * CELLS, up), F32),
            pltpu.VMEM((max(CELLS - late, 16), up), BF), pltpu.VMEM((CELLS, up), BF), pltpu.VMEM((secs, late, up), BF),
            pltpu.VMEM((rows, up), BF), pltpu.VMEM((secs, rows - late, up), BF), pltpu.VMEM((secs, late, up), BF),
            pltpu.VMEM((2, SUB, seq), F32),
            dma, dma, dma, dma, dma((3,)), dma((2,)),
            dma, dma, dma((groups,)), dma((2,)), dma((3,)), dma((2,)), dma((4,)),
        ],
        compiler_params=pltpu.CompilerParams(
            collective_id=0, has_side_effects=True, vmem_limit_bytes=60 << 20
        ),
        name="section_kernel",
    )(clip_frames, destination, timestep, flat(queries), flat(keys), flat(values), flat(hidden), modulation, down_weight, taps)
    return out.reshape(1, rows, up)


def solution(mesh):
    tokens = P("sec", "ctx", None)
    return jax.shard_map(
        body, mesh=mesh, in_specs=(tokens,) * 4 + (P(),) * 6, out_specs=tokens, check_vma=False
    )
```

```python
import functools
import math

import jax
import jax.numpy as jnp
from jax import lax
from jax.experimental import pallas as pl
from jax.experimental.pallas import tpu as pltpu
from jax.sharding import PartitionSpec as P

HEADS = 32
HD = 128
CELLS = 64
SUB = 256
LATE = 32
MESH = pl.DeviceIdType.MESH
BF = jnp.bfloat16
F32 = jnp.float32


def kernel(
    frames_ref, dest_ref, step_ref,
    q_hbm, k_hbm, v_hbm, hid_hbm, mod_hbm, down_hbm, conv_hbm,
    out_ref,
    qf, kf, vf, k2, v2, o_send, att, hid, mod, down, conv, proj, xpad, lohalo, hihalo, last_halo, clip_own, gathered_0, gathered_1, scores,
    send_k, send_v, send_q, send_o, send_h, send_g,
    recv_k, recv_v, recv_q, recv_o, recv_h, recv_g, w_sem,
):
    rows = q_hbm.shape[0]
    ctx = lax.axis_size("ctx")
    secs = lax.axis_size("sec")
    me = lax.axis_index("ctx")
    sec = lax.axis_index("sec")
    below = lax.rem(me + ctx - 1, ctx)
    above = lax.rem(me + 1, ctx)
    zi, yi, ci = me // 4, (me // 2) % 2, me % 2
    parts = ((0, rows - LATE), (rows - LATE, LATE))
    last = len(parts) - 1
    group = 4 * rows
    groups = ctx // 4

    def place(dz, dy, dc):
        return lax.rem(zi + dz, groups) * 4 + lax.rem(yi + dy, 2) * 2 + lax.rem(ci + dc, 2)

    barrier = pltpu.get_barrier_semaphore()

    def greet_ctx(i, carry):
        pl.semaphore_signal(barrier, inc=1, device_id={"ctx": lax.rem(me + i, ctx)}, device_id_type=MESH)
        return carry

    def greet_sec(i, carry):
        for place_at in (me, above, below):
            pl.semaphore_signal(
                barrier, inc=1, device_id={"sec": lax.rem(sec + i, secs), "ctx": place_at}, device_id_type=MESH)
        return carry

    lax.fori_loop(1, ctx, greet_ctx, 0)
    lax.fori_loop(1, secs, greet_sec, 0)
    pl.semaphore_wait(barrier, ctx - 1 + 3 * (secs - 1))

    def offset(k):
        return jnp.where(k == groups - 1, 0, jnp.where(k % 2 == 0, groups - 1 - k // 2, k // 2 + 1))

    my_rows = pl.ds(pl.multiple_of(me * rows, rows), rows)
    my_cols = pl.ds(pl.multiple_of(me * HD, HD), HD)

    def scatter(src, dst, send, recv):
        def one(i, carry):
            dz, j = lax.rem(groups - offset(i // 4), groups), 3 - i % 4
            to = place(dz, j // 2, j % 2)
            cols = pl.ds(pl.multiple_of(to * HD, HD), HD)
            pltpu.make_async_remote_copy(
                src_ref=src.at[:, cols], dst_ref=dst.at[my_rows], send_sem=send, recv_sem=recv,
                device_id={"ctx": to}, device_id_type=MESH,
            ).start()
            return carry

        lax.fori_loop(0, ctx - 1, one, 0)
        pltpu.make_async_copy(src.at[:, my_cols], dst.at[my_rows], recv).start()

    scatter(k_hbm, kf, send_k, recv_k)
    scatter(v_hbm, vf, send_v, recv_v)
    scatter(q_hbm, qf, send_q, recv_q.at[zi])
    loads = [
        pltpu.make_async_copy(a, b, w_sem.at[n])
        for n, (a, b) in enumerate(((hid_hbm, hid), (mod_hbm, mod), (down_hbm, down), (conv_hbm, conv)))
    ]
    for load in loads:
        load.start()

    frames = frames_ref[sec]
    pltpu.make_async_copy(kf, kf, recv_k).wait()
    first = kf[0:1, :]
    key_at = lax.broadcasted_iota(jnp.int32, kf.shape, 0)
    valid = key_at < frames * CELLS
    kk = jnp.where(valid, kf[...].astype(F32), first.astype(F32)).astype(BF)
    k2[:, 0:HD] = kk
    k2[:, HD:] = kk
    pltpu.make_async_copy(vf, vf, recv_v).wait()
    v2[:, 0:HD] = jnp.where(valid, vf[...].astype(F32), 0.0).astype(BF)
    v2[:, HD:] = jnp.where(valid, 1.0, 0.0).astype(BF)

    scale = math.log2(math.e) / math.sqrt(HD)

    def attend(k, carry):
        dz = offset(k)
        g = lax.rem(zi + dz, groups)
        at = pl.ds(pl.multiple_of(g * group, group), group)
        pltpu.make_async_copy(qf.at[at], qf.at[at], recv_q.at[g]).wait()
        start = g * group

        def part(i):
            return pl.ds(pl.multiple_of(start + i * SUB, SUB), SUB)

        def score(i):
            wide = qf[part(i), :].astype(F32) * scale
            high = wide.astype(BF)
            low = (wide - high.astype(F32)).astype(BF)
            q2 = jnp.concatenate([high, low], axis=1)
            return lax.dot_general(q2, k2[...], (((1,), (1,)), ((), ())), preferred_element_type=F32)

        parts = group // SUB
        scores[0] = score(0)
        for i in range(parts):
            if i + 1 < parts:
                scores[(i + 1) % 2] = score(i + 1)
            here = scores[i % 2]
            top = jnp.max(here, axis=1, keepdims=True)
            weights = jnp.exp2(here - top).astype(BF)
            both = jnp.dot(weights, v2[...], preferred_element_type=F32)
            o_send[part(i), :] = (both[:, 0:HD] / both[:, HD:]).astype(BF)
        for j in (3, 2, 1, 0):
            if j:
                give(0, dz, j)
            else:
                pl.when(k < groups - 1)(functools.partial(give, 0, dz, j))
        return carry

    def give(h, dz, j):
        to = place(dz, j // 2, j % 2)
        start, size = parts[h]
        pltpu.make_async_remote_copy(
            src_ref=o_send.at[pl.ds(pl.multiple_of(to * rows + start, 16), size)],
            dst_ref=att.at[pl.ds(start, size), my_cols],
            send_sem=send_o, recv_sem=recv_o.at[h],
            device_id={"ctx": to}, device_id_type=MESH,
        ).start()

    def keep_own(h):
        start, size = parts[h]
        pltpu.make_async_copy(
            o_send.at[pl.ds(pl.multiple_of(me * rows + start, 16), size)],
            att.at[pl.ds(start, size), my_cols], recv_o.at[h]).start()

    lax.fori_loop(0, groups, attend, 0)
    keep_own(0)
    for h in range(1, len(parts)):
        def rest(i, carry, h=h):
            give(h, offset(lax.rem(i, groups)), 3 - i // groups)
            return carry

        lax.fori_loop(0, ctx - 1, rest, 0)
        keep_own(h)

    for load in loads:
        load.wait()
    now = step_ref[sec]
    shift, scale_up, gate = (mod[n, pl.ds(now, 1), :] for n in range(3))
    source = jnp.int32(0)
    for s in range(dest_ref.shape[0]):
        source = jnp.where(dest_ref[s] == sec, s, source)

    def adapt(h):
        start, size = parts[h]
        at = pl.ds(start, size)
        pltpu.make_async_copy(att.at[at], att.at[at], recv_o.at[h]).wait()
        block = (hid[at, :].astype(F32) + gate * att[at, :].astype(F32)).astype(BF)
        wide = block.astype(F32)
        centre = jnp.mean(wide, axis=1, keepdims=True)
        away = wide - centre
        spread = jnp.mean(away * away, axis=1, keepdims=True)
        normed = (away * lax.rsqrt(spread + 1e-06) * (1.0 + scale_up) + shift).astype(BF)
        projected = jnp.dot(normed, down[...], preferred_element_type=F32)
        cell = me * rows + start + lax.broadcasted_iota(jnp.int32, projected.shape, 0)
        proj[at, :] = jnp.where(cell < frames * CELLS, projected, 0.0).astype(BF)

    boxes = (gathered_0, gathered_1)

    def hand_off(h):
        at = pl.ds(*parts[h])

        def one(i, carry):
            pltpu.make_async_remote_copy(
                src_ref=proj.at[at], dst_ref=boxes[h].at[sec], send_sem=send_g.at[h], recv_sem=recv_g.at[h],
                device_id={"sec": lax.rem(sec + lax.rem(i * 3, secs), secs)}, device_id_type=MESH,
            ).start()
            return carry

        def beside(i, carry):
            pltpu.make_async_remote_copy(
                src_ref=proj.at[at], dst_ref=last_halo.at[sec], send_sem=send_h.at[2], recv_sem=recv_h.at[2],
                device_id={"sec": lax.rem(sec + i, secs), "ctx": above}, device_id_type=MESH,
            ).start()
            return carry

        if h == last:
            lax.fori_loop(0, secs, beside, 0)
        lax.fori_loop(1, secs, one, 0)
        pltpu.make_async_copy(proj.at[at], boxes[h].at[sec], recv_g.at[h]).start()

    def take(h):
        pltpu.make_async_copy(boxes[h], boxes[h], recv_g.at[h]).wait()
        clip_own[pl.ds(*parts[h]), :] = boxes[h][source]

    before = CELLS - LATE
    dn = pltpu.make_async_remote_copy(
        src_ref=clip_own.at[pl.ds(0, CELLS)], dst_ref=hihalo, send_sem=send_h.at[0], recv_sem=recv_h.at[0],
        device_id={"ctx": below}, device_id_type=MESH)
    up = before and pltpu.make_async_remote_copy(
        src_ref=clip_own.at[pl.ds(rows - CELLS, before)], dst_ref=lohalo, send_sem=send_h.at[1], recv_sem=recv_h.at[1],
        device_id={"ctx": above}, device_id_type=MESH)

    adapt(0)
    hand_off(0)
    adapt(1)
    hand_off(1)
    take(0)
    dn.start()
    if before:
        up.start()
    take(1)
    dn.wait_recv()
    if before:
        up.wait_recv()
    pltpu.make_async_copy(last_halo, last_halo, recv_h.at[2]).wait()

    total_rows = rows + 2 * CELLS
    clip = clip_own[...].astype(F32)
    if before:
        xpad[0:before, :] = jnp.where(me > 0, lohalo[...].astype(F32), 0.0)
    xpad[before:CELLS, :] = jnp.where(me > 0, last_halo[source].astype(F32), 0.0)
    xpad[CELLS:CELLS + rows, :] = clip
    xpad[CELLS + rows:, :] = jnp.where(me < ctx - 1, hihalo[...].astype(F32), 0.0)
    padded = xpad[...]
    at = lax.broadcasted_iota(jnp.int32, padded.shape, 0) % CELLS
    row, col = at // 8, at % 8
    total = clip
    for b in range(3):
        for e in range(3):
            step = (b - 1) * 8 + (e - 1)
            moved = padded if step == 0 else pltpu.roll(padded, (-step) % total_rows, 0)
            inside = (row + b - 1 >= 0) & (row + b - 1 < 8) & (col + e - 1 >= 0) & (col + e - 1 < 8)
            moved = jnp.where(inside, moved, 0.0).astype(BF)
            for a in range(3):
                total += jnp.dot(moved[a * CELLS:a * CELLS + rows], conv[a * 9 + b * 3 + e], preferred_element_type=F32)
    cell = me * rows + lax.broadcasted_iota(jnp.int32, total.shape, 0)
    out_ref[...] = jnp.where(cell < frames_ref[source] * CELLS, total, 0.0).astype(BF)

    others = pl.ds(0, (ctx - 1) * rows)
    pltpu.make_async_copy(kf.at[others], kf.at[others], send_k).wait()
    pltpu.make_async_copy(vf.at[others], vf.at[others], send_v).wait()
    pltpu.make_async_copy(qf.at[others], qf.at[others], send_q).wait()
    pltpu.make_async_copy(o_send.at[others], o_send.at[others], send_o).wait()
    dn.wait_send()
    if before:
        up.wait_send()
    pltpu.make_async_copy(last_halo, last_halo, send_h.at[2]).wait()
    sent = pl.ds(0, secs - 1)
    for h, box in enumerate(boxes):
        pltpu.make_async_copy(box.at[sent], box.at[sent], send_g.at[h]).wait()


def body(hidden, queries, keys, values, modulation, down_weight, conv_weight, clip_frames, destination, timestep):
    _, rows, width = queries.shape
    seq = rows * lax.axis_size("ctx")
    secs = lax.axis_size("sec")
    groups = lax.axis_size("ctx") // 4
    up = down_weight.shape[1]
    late = min(LATE, CELLS)
    flat = lambda t: t.reshape(rows, width)
    smem = pl.BlockSpec(memory_space=pltpu.SMEM)
    anywhere = pl.BlockSpec(memory_space=pl.ANY)
    dma = pltpu.SemaphoreType.DMA
    taps = conv_weight.reshape(27, up, up)
    modulation = jnp.swapaxes(modulation, 0, 1)
    out = pl.pallas_call(
        kernel,
        out_shape=jax.ShapeDtypeStruct((rows, up), BF),
        in_specs=[smem] * 3 + [anywhere] * 7,
        out_specs=pl.BlockSpec(memory_space=pltpu.VMEM),
        scratch_shapes=[
            pltpu.VMEM((seq, HD), BF), pltpu.VMEM((seq, HD), BF), pltpu.VMEM((seq, HD), BF),
            pltpu.VMEM((seq, 2 * HD), BF), pltpu.VMEM((seq, 2 * HD), BF),
            pltpu.VMEM((seq, HD), BF), pltpu.VMEM((rows, width), BF), pltpu.VMEM((rows, width), BF),
            pltpu.VMEM(modulation.shape, F32), pltpu.VMEM(down_weight.shape, BF), pltpu.VMEM(taps.shape, BF),
            pltpu.VMEM((rows, up), BF), pltpu.VMEM((rows + 2 * CELLS, up), F32),
            pltpu.VMEM((max(CELLS - late, 16), up), BF), pltpu.VMEM((CELLS, up), BF), pltpu.VMEM((secs, late, up), BF),
            pltpu.VMEM((rows, up), BF), pltpu.VMEM((secs, rows - late, up), BF), pltpu.VMEM((secs, late, up), BF),
            pltpu.VMEM((2, SUB, seq), F32),
            dma, dma, dma, dma, dma((3,)), dma((2,)),
            dma, dma, dma((groups,)), dma((2,)), dma((3,)), dma((2,)), dma((4,)),
        ],
        compiler_params=pltpu.CompilerParams(
            collective_id=0, has_side_effects=True, vmem_limit_bytes=60 << 20
        ),
        name="section_kernel",
    )(clip_frames, destination, timestep, flat(queries), flat(keys), flat(values), flat(hidden), modulation, down_weight, taps)
    return out.reshape(1, rows, up)


def solution(mesh):
    tokens = P("sec", "ctx", None)
    return jax.shard_map(
        body, mesh=mesh, in_specs=(tokens,) * 4 + (P(),) * 6, out_specs=tokens, check_vma=False
    )
```

```python
import functools
import math

import jax
import jax.numpy as jnp
from jax import lax
from jax.experimental import pallas as pl
from jax.experimental.pallas import tpu as pltpu
from jax.sharding import PartitionSpec as P

HEADS = 32
HD = 128
CELLS = 64
SUB = 256
LATE = 32
MESH = pl.DeviceIdType.MESH
BF = jnp.bfloat16
F32 = jnp.float32


def kernel(
    frames_ref, dest_ref, step_ref,
    q_hbm, k_hbm, v_hbm, hid_hbm, mod_hbm, down_hbm, conv_hbm,
    out_ref,
    qf, kf, vf, k2, v2, o_send, att, hid, mod, down, conv, proj, xpad, lohalo, hihalo, last_halo, clip_own, gathered_0, gathered_1, scores,
    send_k, send_v, send_q, send_o, send_h, send_g,
    recv_k, recv_v, recv_q, recv_o, recv_h, recv_g, w_sem,
):
    rows = q_hbm.shape[0]
    ctx = lax.axis_size("ctx")
    secs = lax.axis_size("sec")
    me = lax.axis_index("ctx")
    sec = lax.axis_index("sec")
    below = lax.rem(me + ctx - 1, ctx)
    above = lax.rem(me + 1, ctx)
    zi, yi, ci = me // 4, (me // 2) % 2, me % 2
    parts = ((0, rows - LATE), (rows - LATE, LATE))
    last = len(parts) - 1
    group = 4 * rows
    groups = ctx // 4

    def place(dz, dy, dc):
        return lax.rem(zi + dz, groups) * 4 + lax.rem(yi + dy, 2) * 2 + lax.rem(ci + dc, 2)

    barrier = pltpu.get_barrier_semaphore()

    def greet_ctx(i, carry):
        pl.semaphore_signal(barrier, inc=1, device_id={"ctx": lax.rem(me + i, ctx)}, device_id_type=MESH)
        return carry

    def greet_sec(i, carry):
        for place_at in (me, below):
            pl.semaphore_signal(
                barrier, inc=1, device_id={"sec": lax.rem(sec + i, secs), "ctx": place_at}, device_id_type=MESH)
        return carry

    lax.fori_loop(1, ctx, greet_ctx, 0)
    lax.fori_loop(1, secs, greet_sec, 0)
    pl.semaphore_wait(barrier, ctx - 1 + 2 * (secs - 1))

    def offset(k):
        return jnp.where(k == groups - 1, 0, jnp.where(k % 2 == 0, groups - 1 - k // 2, k // 2 + 1))

    my_rows = pl.ds(pl.multiple_of(me * rows, rows), rows)
    my_cols = pl.ds(pl.multiple_of(me * HD, HD), HD)

    def scatter(src, dst, send, recv):
        def one(i, carry):
            dz, j = lax.rem(groups - offset(i // 4), groups), 3 - i % 4
            to = place(dz, j // 2, j % 2)
            cols = pl.ds(pl.multiple_of(to * HD, HD), HD)
            pltpu.make_async_remote_copy(
                src_ref=src.at[:, cols], dst_ref=dst.at[my_rows], send_sem=send, recv_sem=recv,
                device_id={"ctx": to}, device_id_type=MESH,
            ).start()
            return carry

        lax.fori_loop(0, ctx - 1, one, 0)
        pltpu.make_async_copy(src.at[:, my_cols], dst.at[my_rows], recv).start()

    scatter(k_hbm, kf, send_k, recv_k)
    scatter(v_hbm, vf, send_v, recv_v)
    scatter(q_hbm, qf, send_q, recv_q.at[zi])
    loads = [
        pltpu.make_async_copy(a, b, w_sem.at[n])
        for n, (a, b) in enumerate(((hid_hbm, hid), (mod_hbm, mod), (down_hbm, down), (conv_hbm, conv)))
    ]
    for load in loads:
        load.start()

    frames = frames_ref[sec]
    pltpu.make_async_copy(kf, kf, recv_k).wait()
    first = kf[0:1, :]
    key_at = lax.broadcasted_iota(jnp.int32, kf.shape, 0)
    valid = key_at < frames * CELLS
    kk = jnp.where(valid, kf[...].astype(F32), first.astype(F32)).astype(BF)
    k2[:, 0:HD] = kk
    k2[:, HD:] = kk
    pltpu.make_async_copy(vf, vf, recv_v).wait()
    v2[:, 0:HD] = jnp.where(valid, vf[...].astype(F32), 0.0).astype(BF)
    v2[:, HD:] = jnp.where(valid, 1.0, 0.0).astype(BF)

    scale = math.log2(math.e) / math.sqrt(HD)

    def attend(k, carry):
        dz = offset(k)
        g = lax.rem(zi + dz, groups)
        at = pl.ds(pl.multiple_of(g * group, group), group)
        pltpu.make_async_copy(qf.at[at], qf.at[at], recv_q.at[g]).wait()
        start = g * group

        def part(i):
            return pl.ds(pl.multiple_of(start + i * SUB, SUB), SUB)

        def score(i):
            wide = qf[part(i), :].astype(F32) * scale
            high = wide.astype(BF)
            low = (wide - high.astype(F32)).astype(BF)
            q2 = jnp.concatenate([high, low], axis=1)
            return lax.dot_general(q2, k2[...], (((1,), (1,)), ((), ())), preferred_element_type=F32)

        parts = group // SUB
        scores[0] = score(0)
        for i in range(parts):
            if i + 1 < parts:
                scores[(i + 1) % 2] = score(i + 1)
            here = scores[i % 2]
            top = jnp.max(here, axis=1, keepdims=True)
            weights = jnp.exp2(here - top).astype(BF)
            both = jnp.dot(weights, v2[...], preferred_element_type=F32)
            o_send[part(i), :] = (both[:, 0:HD] / both[:, HD:]).astype(BF)
        for j in (3, 2, 1, 0):
            if j:
                give(0, dz, j)
            else:
                pl.when(k < groups - 1)(functools.partial(give, 0, dz, j))
        return carry

    def give(h, dz, j):
        to = place(dz, j // 2, j % 2)
        start, size = parts[h]
        pltpu.make_async_remote_copy(
            src_ref=o_send.at[pl.ds(pl.multiple_of(to * rows + start, 16), size)],
            dst_ref=att.at[pl.ds(start, size), my_cols],
            send_sem=send_o, recv_sem=recv_o.at[h],
            device_id={"ctx": to}, device_id_type=MESH,
        ).start()

    def keep_own(h):
        start, size = parts[h]
        pltpu.make_async_copy(
            o_send.at[pl.ds(pl.multiple_of(me * rows + start, 16), size)],
            att.at[pl.ds(start, size), my_cols], recv_o.at[h]).start()

    lax.fori_loop(0, groups, attend, 0)
    keep_own(0)
    for h in range(1, len(parts)):
        def rest(i, carry, h=h):
            give(h, offset(lax.rem(i, groups)), 3 - i // groups)
            return carry

        lax.fori_loop(0, ctx - 1, rest, 0)
        keep_own(h)

    for load in loads:
        load.wait()
    now = step_ref[sec]
    shift, scale_up, gate = (mod[n, pl.ds(now, 1), :] for n in range(3))
    source = jnp.int32(0)
    for s in range(dest_ref.shape[0]):
        source = jnp.where(dest_ref[s] == sec, s, source)

    def adapt(h):
        start, size = parts[h]
        at = pl.ds(start, size)
        pltpu.make_async_copy(att.at[at], att.at[at], recv_o.at[h]).wait()
        block = (hid[at, :].astype(F32) + gate * att[at, :].astype(F32)).astype(BF)
        wide = block.astype(F32)
        centre = jnp.mean(wide, axis=1, keepdims=True)
        away = wide - centre
        spread = jnp.mean(away * away, axis=1, keepdims=True)
        normed = (away * lax.rsqrt(spread + 1e-06) * (1.0 + scale_up) + shift).astype(BF)
        projected = jnp.dot(normed, down[...], preferred_element_type=F32)
        cell = me * rows + start + lax.broadcasted_iota(jnp.int32, projected.shape, 0)
        proj[at, :] = jnp.where(cell < frames * CELLS, projected, 0.0).astype(BF)

    boxes = (gathered_0, gathered_1)

    def hand_off(h):
        at = pl.ds(*parts[h])

        def one(i, carry):
            pltpu.make_async_remote_copy(
                src_ref=proj.at[at], dst_ref=boxes[h].at[sec], send_sem=send_g.at[h], recv_sem=recv_g.at[h],
                device_id={"sec": lax.rem(sec + lax.rem(i * 3, secs), secs)}, device_id_type=MESH,
            ).start()
            return carry

        def beside(i, carry):
            pltpu.make_async_remote_copy(
                src_ref=proj.at[at], dst_ref=last_halo.at[sec], send_sem=send_h.at[2], recv_sem=recv_h.at[2],
                device_id={"sec": lax.rem(sec + i, secs), "ctx": above}, device_id_type=MESH,
            ).start()
            return carry

        if h == last:
            lax.fori_loop(0, secs, beside, 0)
        lax.fori_loop(1, secs, one, 0)
        pltpu.make_async_copy(proj.at[at], boxes[h].at[sec], recv_g.at[h]).start()

    def take(h):
        pltpu.make_async_copy(boxes[h], boxes[h], recv_g.at[h]).wait()
        clip_own[pl.ds(*parts[h]), :] = boxes[h][source]

    before = CELLS - LATE
    dn = pltpu.make_async_remote_copy(
        src_ref=clip_own.at[pl.ds(0, CELLS)], dst_ref=hihalo, send_sem=send_h.at[0], recv_sem=recv_h.at[0],
        device_id={"ctx": below}, device_id_type=MESH)
    up = before and pltpu.make_async_remote_copy(
        src_ref=clip_own.at[pl.ds(rows - CELLS, before)], dst_ref=lohalo, send_sem=send_h.at[1], recv_sem=recv_h.at[1],
        device_id={"ctx": above}, device_id_type=MESH)

    adapt(0)
    hand_off(0)
    adapt(1)
    hand_off(1)
    take(0)
    dn.start()
    if before:
        up.start()
    take(1)
    dn.wait_recv()
    if before:
        up.wait_recv()
    pltpu.make_async_copy(last_halo, last_halo, recv_h.at[2]).wait()

    total_rows = rows + 2 * CELLS
    clip = clip_own[...].astype(F32)
    if before:
        xpad[0:before, :] = jnp.where(me > 0, lohalo[...].astype(F32), 0.0)
    xpad[before:CELLS, :] = jnp.where(me > 0, last_halo[source].astype(F32), 0.0)
    xpad[CELLS:CELLS + rows, :] = clip
    xpad[CELLS + rows:, :] = jnp.where(me < ctx - 1, hihalo[...].astype(F32), 0.0)
    padded = xpad[...]
    at = lax.broadcasted_iota(jnp.int32, padded.shape, 0) % CELLS
    row, col = at // 8, at % 8
    total = clip
    for b in range(3):
        for e in range(3):
            step = (b - 1) * 8 + (e - 1)
            moved = padded if step == 0 else pltpu.roll(padded, (-step) % total_rows, 0)
            inside = (row + b - 1 >= 0) & (row + b - 1 < 8) & (col + e - 1 >= 0) & (col + e - 1 < 8)
            moved = jnp.where(inside, moved, 0.0).astype(BF)
            for a in range(3):
                total += jnp.dot(moved[a * CELLS:a * CELLS + rows], conv[a * 9 + b * 3 + e], preferred_element_type=F32)
    cell = me * rows + lax.broadcasted_iota(jnp.int32, total.shape, 0)
    out_ref[...] = jnp.where(cell < frames_ref[source] * CELLS, total, 0.0).astype(BF)

    others = pl.ds(0, (ctx - 1) * rows)
    pltpu.make_async_copy(kf.at[others], kf.at[others], send_k).wait()
    pltpu.make_async_copy(vf.at[others], vf.at[others], send_v).wait()
    pltpu.make_async_copy(qf.at[others], qf.at[others], send_q).wait()
    pltpu.make_async_copy(o_send.at[others], o_send.at[others], send_o).wait()
    dn.wait_send()
    if before:
        up.wait_send()
    pltpu.make_async_copy(last_halo, last_halo, send_h.at[2]).wait()
    sent = pl.ds(0, secs - 1)
    for h, box in enumerate(boxes):
        pltpu.make_async_copy(box.at[sent], box.at[sent], send_g.at[h]).wait()


def body(hidden, queries, keys, values, modulation, down_weight, conv_weight, clip_frames, destination, timestep):
    _, rows, width = queries.shape
    seq = rows * lax.axis_size("ctx")
    secs = lax.axis_size("sec")
    groups = lax.axis_size("ctx") // 4
    up = down_weight.shape[1]
    late = min(LATE, CELLS)
    flat = lambda t: t.reshape(rows, width)
    smem = pl.BlockSpec(memory_space=pltpu.SMEM)
    anywhere = pl.BlockSpec(memory_space=pl.ANY)
    dma = pltpu.SemaphoreType.DMA
    taps = conv_weight.reshape(27, up, up)
    modulation = jnp.swapaxes(modulation, 0, 1)
    out = pl.pallas_call(
        kernel,
        out_shape=jax.ShapeDtypeStruct((rows, up), BF),
        in_specs=[smem] * 3 + [anywhere] * 7,
        out_specs=pl.BlockSpec(memory_space=pltpu.VMEM),
        scratch_shapes=[
            pltpu.VMEM((seq, HD), BF), pltpu.VMEM((seq, HD), BF), pltpu.VMEM((seq, HD), BF),
            pltpu.VMEM((seq, 2 * HD), BF), pltpu.VMEM((seq, 2 * HD), BF),
            pltpu.VMEM((seq, HD), BF), pltpu.VMEM((rows, width), BF), pltpu.VMEM((rows, width), BF),
            pltpu.VMEM(modulation.shape, F32), pltpu.VMEM(down_weight.shape, BF), pltpu.VMEM(taps.shape, BF),
            pltpu.VMEM((rows, up), BF), pltpu.VMEM((rows + 2 * CELLS, up), F32),
            pltpu.VMEM((max(CELLS - late, 16), up), BF), pltpu.VMEM((CELLS, up), BF), pltpu.VMEM((secs, late, up), BF),
            pltpu.VMEM((rows, up), BF), pltpu.VMEM((secs, rows - late, up), BF), pltpu.VMEM((secs, late, up), BF),
            pltpu.VMEM((2, SUB, seq), F32),
            dma, dma, dma, dma, dma((3,)), dma((2,)),
            dma, dma, dma((groups,)), dma((2,)), dma((3,)), dma((2,)), dma((4,)),
        ],
        compiler_params=pltpu.CompilerParams(
            collective_id=0, has_side_effects=True, vmem_limit_bytes=60 << 20
        ),
        name="section_kernel",
    )(clip_frames, destination, timestep, flat(queries), flat(keys), flat(values), flat(hidden), modulation, down_weight, taps)
    return out.reshape(1, rows, up)


def solution(mesh):
    tokens = P("sec", "ctx", None)
    return jax.shard_map(
        body, mesh=mesh, in_specs=(tokens,) * 4 + (P(),) * 6, out_specs=tokens, check_vma=False
    )
```
